32 devices in a mesh: group: 2 (over y), slab: 4 (over z), plane: 4 (over x, core).
Axes of the slice: x: 2, y: 2, z: 4, core: 2. Of those that a mesh axis runs over, the one named last changes fastest.
Arguments:
- fields: float32 [2, 32, 128, 1024], P('group', None, 'slab', 'plane'), may hold values from 0 to 2
- evap_rates: float32 [32], replicated, may hold values from 0.05 to 0.5
- coal_kernel: bfloat16 [32, 1024], replicated, may hold values from -0.1875 to 0.1875
- plume_width: float32 [8], replicated, may hold values from 1 to 8
- owner_map: int32 [16, 2048], P(('slab', 'plane')), may hold values from 0 to 15, as said below
- deposit_cell: int32 [16, 2048], P(('slab', 'plane')), may hold values from 0 to 8191
- plume_ids: int32 [16, 2048], P(('slab', 'plane')), may hold values from 0 to 7
Outputs:
- new_fields: float32 [2, 32, 128, 1024], P('group', None, 'slab', 'plane')
The draws below stay inside these ranges and needn't reach their ends.
Inputs may be any that keep to these rules, and one draw needn't show every extreme that they name: `owner_map`: among the 2048 rows of one index of the first dimension, at most 256 name any one spray block, and one block is named by exactly 256 of them at every index.
All inputs are finite; a program needn't handle non-finite values.
Results may differ from the reference program's by a relative error of at most 0.0014.
Values may be sent and summed in bfloat16 or wider, within the bound.
A program may use at most 64 MiB of HBM per device.

```python
import math
import jax
import jax.numpy as jnp
import numpy as np
from jax import lax

SEC = 32
PLUMES = 8
CA = 32
CB = 256
NA = 128
NB = 1024
OWNERS = 16
EXIT_ROWS = 2048
CAP = 256
N_SLAB = 4
N_PLANE = 4


def draw_owner_map(key, part):
    key_hot, key_order, key_rows = jax.random.split(key, 3)
    hottest = jax.random.randint(key_hot, (), 0, OWNERS).astype(jnp.int32)
    labels = jax.random.permutation(key_order, OWNERS - 1).astype(jnp.int32)
    others = jnp.where(labels >= hottest, labels + 1, labels).astype(jnp.int32)
    heavy = OWNERS // 2
    pool_index = np.concatenate([np.repeat(np.arange(heavy), CAP), np.repeat(np.arange(heavy, OWNERS - 1), CAP // 4)]).astype(np.int32)
    slot_pool = others[pool_index]

    def draw_block(block_key):
        key_pick, key_place = jax.random.split(block_key)
        chosen = jax.random.permutation(key_pick, slot_pool)[:EXIT_ROWS - CAP]
        listing = jnp.concatenate([jnp.full((CAP,), hottest, jnp.int32), chosen.astype(jnp.int32)])
        return jax.random.permutation(key_place, listing)
    return jax.vmap(draw_block)(jax.random.split(key_rows, OWNERS))


def set_ends(array, own_key, least, top_value):
    dims = array.shape
    place = [jax.random.randint(jax.random.fold_in(own_key, axis), (), 0, dims[axis]) for axis in range(len(dims))]
    array = array.at[tuple(place)].set(least)
    longest = dims.index(max(dims))
    place[longest] = (place[longest] + 1) % dims[longest]
    return array.at[tuple(place)].set(top_value)


def level_of(key, shape, shards, least, top_value):
    def one(dim, shards_of):
        heights = jax.random.uniform(jax.random.fold_in(jax.random.fold_in(key, 6), dim), (shards_of,), jnp.float32, least / len(shards), top_value / len(shards))
        return jnp.repeat(jnp.exp(heights), shape[dim] // shards_of).reshape((-1,) + (1,) * (len(shape) - dim - 1))

    gain = one(*shards[0])
    for cut in shards[1:]:
        gain = gain * one(*cut)
    return gain


def scatter_about(stream_key, extent, deviation, bound, kind=jnp.bfloat16):
    return jnp.clip(deviation * jax.random.normal(stream_key, extent, jnp.float32), -bound, bound).astype(kind)


def setup_inputs(seed: int = 0) -> dict:
    arg_keys = jax.random.split(jax.random.key(seed), 8)
    fields = jnp.clip(2.0 * jax.random.uniform(arg_keys[0], (2, SEC, NA, NB), jnp.float32) ** level_of(arg_keys[0], (2, SEC, NA, NB), ((0, 2), (2, 4), (3, 4)), -0.2, 0.2), 0.0, 2.0)
    evap_rates = jnp.clip(jnp.exp(jax.random.uniform(arg_keys[1], (SEC,), jnp.float32, math.log(0.05), math.log(0.5))), 0.05, 0.5)
    coal_kernel = scatter_about(arg_keys[2], (SEC, SEC * SEC), (SEC * SEC) ** -0.5, 0.1875)
    plume_width = jnp.clip(jnp.exp(jax.random.uniform(arg_keys[3], (PLUMES,), jnp.float32, math.log(1.0), math.log(8.0))), 1.0, 8.0)
    owner_map = draw_owner_map(jax.random.fold_in(arg_keys[7], 71), 0)
    deposit_cell = set_ends(jax.random.randint(arg_keys[5], (OWNERS, EXIT_ROWS), 0, CA * CB), jax.random.fold_in(arg_keys[5], 1), 0, (CA * CB) - 1).astype(jnp.int32)
    plume_ids = set_ends(jax.random.randint(arg_keys[6], (OWNERS, EXIT_ROWS), 0, PLUMES), jax.random.fold_in(arg_keys[6], 1), 0, PLUMES - 1).astype(jnp.int32)
    return dict(fields=fields, evap_rates=evap_rates, coal_kernel=coal_kernel, plume_width=plume_width, owner_map=owner_map, deposit_cell=deposit_cell, plume_ids=plume_ids)


cfl_nozzle = 0.35
diffusion = 0.2
relax_rate = 5.0
relax_step = 0.1
collide_step = 0.25

def laplace(padded):
    center = padded[:, 1:-1, 1:-1]
    return padded[:, :-2, 1:-1] + padded[:, 2:, 1:-1] + padded[:, 1:-1, :-2] + padded[:, 1:-1, 2:] - 4.0 * center

def nozzle_update(padded):
    center = padded[:, 1:-1, 1:-1]
    channels, span_axial, span_cross = center.shape
    layers = channels // 4
    blocks = center.reshape(4, layers, span_axial, span_cross)
    spread = laplace(padded).reshape(4, layers, span_axial, span_cross)
    previous = jnp.concatenate([jnp.zeros_like(blocks[:, :1]), blocks[:, :-1]], axis=1)
    upwind = blocks - previous
    density = blocks[0]
    mass_flux = blocks[1]
    quality = blocks[2]
    enthalpy = blocks[3]
    relaxing = relax_rate / (1.0 + density * density)
    new_density = density - cfl_nozzle * upwind[1] + diffusion * spread[0]
    new_flux = mass_flux - cfl_nozzle * (upwind[1] + upwind[2]) + diffusion * spread[1]
    new_quality = quality + relax_step * relaxing * (enthalpy - quality) - cfl_nozzle * upwind[2] + diffusion * spread[2]
    new_enthalpy = enthalpy - cfl_nozzle * upwind[3] + diffusion * spread[3]
    stacked = jnp.stack([new_density, new_flux, new_quality, new_enthalpy])
    return stacked.reshape(channels, span_axial, span_cross)

def spray_transport(padded, evap_rates):
    center = padded[:, 1:-1, 1:-1]
    sections = center.shape[0]
    speeds = 0.2 + 0.5 * jnp.arange(sections, dtype=jnp.float32) / (sections - 1)
    shifted = center - speeds[:, None, None] * (center - padded[:, :-2, 1:-1]) + diffusion * laplace(padded)
    evaporated = evap_rates[:, None, None] * center
    gained = jnp.concatenate([evaporated[1:], jnp.zeros_like(evaporated[:1])], axis=0)
    return shifted - evaporated + gained

def collide(flattened, coal_kernel):
    sections, cell_count = flattened.shape
    block_size = min(2048, cell_count)
    pieces = flattened.reshape(sections, cell_count // block_size, block_size).transpose(1, 0, 2)
    kernel_wide = coal_kernel.astype(jnp.float32)

    def collide_block(segment):
        pair_terms = (segment[:, None, :] * segment[None, :, :]).reshape(sections * sections, block_size)
        pair_terms = pair_terms.astype(jnp.bfloat16).astype(jnp.float32)
        return jnp.dot(kernel_wide, pair_terms, precision=lax.Precision.HIGHEST)
    return lax.map(collide_block, pieces).transpose(1, 0, 2).reshape(sections, cell_count)

def spray_update(padded, evap_rates, coal_kernel):
    shifted = spray_transport(padded, evap_rates)
    sections, span_axial, span_cross = shifted.shape
    flattened = shifted.reshape(sections, span_axial * span_cross)
    midpoint = flattened + 0.5 * collide_step * collide(flattened, coal_kernel)
    advanced = flattened + collide_step * collide(midpoint, coal_kernel)
    return advanced.reshape(sections, span_axial, span_cross)

def row_masses(coarse, plume_ids, plume_width):
    mass_flux = coarse[1]
    quality = coarse[2]
    enthalpy = coarse[3]
    strength = jnp.sqrt(1.0 + mass_flux * mass_flux)
    center = (SEC - 1) * jax.nn.sigmoid(enthalpy - 2.0 * quality)
    matches = plume_ids[:, None] == jnp.arange(plume_width.shape[0], dtype=jnp.int32)[None, :]
    spread_width = lax.optimization_barrier(jnp.sum(jnp.where(matches, plume_width[None, :], 0.0), axis=1))
    levels = jnp.arange(SEC, dtype=jnp.float32)
    scaled = (levels[:, None] - center[None, :]) / spread_width[None, :]
    weights = 1.0 / (1.0 + scaled * scaled)
    masses = strength[None, :] * weights / lax.optimization_barrier(jnp.sum(weights, axis=0, keepdims=True))
    return masses.astype(jnp.bfloat16)

def reference(fields, evap_rates, coal_kernel, plume_width, owner_map, deposit_cell, plume_ids):
    widths = ((0, 0), (1, 1), (1, 1))
    nozzle = nozzle_update(jnp.pad(fields[0], widths))
    spray_field = spray_update(jnp.pad(fields[1], widths), evap_rates, coal_kernel)
    layers = SEC // 4
    exit_layer = nozzle.reshape(4, layers, NA, NB)[:, layers - 1]
    coarse = exit_layer.reshape(4, NA // 2, 2, NB // 2, 2).mean(axis=(2, 4))
    coarse = coarse.reshape(4, N_SLAB, CA // 2, N_PLANE, CB // 2).transpose(0, 1, 3, 2, 4)
    coarse = coarse.reshape(4, OWNERS * EXIT_ROWS)
    masses = row_masses(coarse, plume_ids.reshape(-1), plume_width)
    owners = owner_map.reshape(-1)
    target_cells = deposit_cell.reshape(-1)
    target_axial = owners // N_PLANE * CA + target_cells // CB
    target_cross = owners % N_PLANE * CB + target_cells % CB
    deposit = jnp.zeros((SEC, NA, NB), jnp.float32).at[:, target_axial, target_cross].add(masses.astype(jnp.float32))
    return jnp.stack([nozzle, spray_field + deposit])
```

```python
import functools

import jax
import jax.numpy as jnp
import numpy as np
from jax import lax
from jax.experimental import pallas as pl
from jax.experimental.pallas import tpu as pltpu
from jax.sharding import PartitionSpec as P

MESH = pl.DeviceIdType.MESH
F32 = jnp.float32
BF16 = jnp.bfloat16
LANES = 128
SLOTS = 256
CHUNK = 2
SOURCES = 4

cfl_nozzle = 0.35
diffusion = 0.2
relax_rate = 5.0
relax_step = 0.1
collide_step = 0.25


def fold_matrix(sections):
    kept = [(i, j) for i in range(sections) for j in range(i // 8 * 8, sections)]
    fold = np.zeros((sections * sections, len(kept)), np.float32)
    for q, (i, j) in enumerate(kept):
        fold[i * sections + j, q] = 1.0
        if j // 8 > i // 8:
            fold[j * sections + i, q] = 1.0
    return fold


def pair_terms(m):
    sections, width = m.shape
    pieces = []
    for i in range(sections):
        low = i // 8 * 8
        pieces.append(jnp.broadcast_to(m[i : i + 1], (sections - low, width)) * m[low:])
    return jnp.concatenate(pieces, axis=0).astype(BF16)


def split_hi_lo(x):
    hi = x.astype(BF16)
    lo = (x - hi.astype(F32)).astype(BF16)
    return hi, lo


def dot_last(a, b):
    return lax.dot_general(a, b, (((1,), (1,)), ((), ())), preferred_element_type=F32)


def kernel(
    n_slab, n_plane, sections, ca, cb, exit_rows,
    fields_hbm, evap_ref, coal_ref, fold_hbm, width_ref, owner_ref, cell_ref, pid_ref,
    out_hbm,
    fbuf, tbuf, hbuf, obuf, fold, cols_out, cols_in, par, send_buf, recv_buf,
    in_sem, out_sem, fold_sem, halo_send, halo_recv, row_send, row_recv,
):
    owners = n_slab * n_plane
    plumes = width_ref.shape[0]
    rows = sections * ca
    g = lax.axis_index("group")
    s = lax.axis_index("slab")
    p = lax.axis_index("plane")
    me = s * n_plane + p

    loads = [
        pltpu.make_async_copy(
            fields_hbm.at[0, :, pl.ds(h * LANES, LANES)], fbuf.at[h], in_sem.at[h]
        )
        for h in range(2)
    ]
    for load in loads:
        load.start()
    fold_load = pltpu.make_async_copy(fold_hbm, fold, fold_sem)

    @pl.when(g == 1)
    def _():
        fold_load.start()

    barrier = pltpu.get_barrier_semaphore()
    sides = [
        (s > 0, (g, s - 1, p)),
        (s < n_slab - 1, (g, s + 1, p)),
        (p > 0, (g, s, p - 1)),
        (p < n_plane - 1, (g, s, p + 1)),
    ]
    near = 0
    for there, target in sides:
        near = near + there.astype(jnp.int32)

        @pl.when(there)
        def _():
            pl.semaphore_signal(barrier, inc=1, device_id=target, device_id_type=MESH)

    @pl.when(g == 1)
    def _():
        @pl.loop(0, owners)
        def _(o):
            pl.semaphore_signal(
                barrier, inc=1, device_id=(0, o // n_plane, o % n_plane), device_id_type=MESH
            )

    pl.semaphore_wait(barrier, near + jnp.where(g == 0, owners, 0))

    for load in loads:
        load.wait()

    def gather_row(ref, a):
        return jnp.concatenate(
            [ref[h, pl.ds(a, sections, stride=ca), :] for h in range(2)], axis=1
        )

    for a in (0, ca - 1):
        tbuf[a + 1] = gather_row(fbuf, a)

    lane = lax.broadcasted_iota(jnp.int32, (8, LANES), 1)
    for h, at in ((0, 0), (1, LANES - 1)):
        select = (lane == at).astype(BF16)
        hi, lo = split_hi_lo(fbuf[h])
        cols_out[h] = (dot_last(select, hi) + dot_last(select, lo))[0:1]

    def halo(kind, target):
        source, landing = (
            (tbuf.at[ca], tbuf.at[0]),
            (tbuf.at[1], tbuf.at[ca + 1]),
            (cols_out.at[1], cols_in.at[0]),
            (cols_out.at[0], cols_in.at[1]),
        )[kind]
        return pltpu.make_async_remote_copy(
            src_ref=source,
            dst_ref=landing,
            send_sem=halo_send.at[kind],
            recv_sem=halo_recv.at[kind],
            device_id=target,
            device_id_type=MESH,
        )

    outgoing = (sides[1], sides[0], sides[3], sides[2])
    for kind in range(4):
        there, target = outgoing[kind]

        @pl.when(there)
        def _():
            halo(kind, target).start()

    @pl.loop(1, ca - 1)
    def _(a):
        tbuf[a + 1] = gather_row(fbuf, a)

    for kind, landing in enumerate((tbuf.at[0], tbuf.at[ca + 1], cols_in.at[0], cols_in.at[1])):

        @pl.when(jnp.logical_not(sides[kind][0]))
        def _():
            landing[...] = jnp.zeros(landing.shape, F32)

    def finish_halo():
        for kind in range(4):

            @pl.when(outgoing[kind][0])
            def _():
                halo(kind, outgoing[kind][1]).wait_send()

            @pl.when(sides[kind][0])
            def _():
                halo(kind, outgoing[kind][1]).wait_recv()

        sub = lax.broadcasted_iota(jnp.int32, (16, LANES), 0)
        lanes = lax.broadcasted_iota(jnp.int32, (16, LANES), 1)
        for h, at in ((0, 0), (1, LANES - 1)):
            hi = cols_in[h].astype(BF16).astype(F32)
            lo = cols_in[h] - hi
            stack = jnp.concatenate([hi, lo, jnp.zeros((14, rows), F32)], axis=0)
            place = jnp.logical_and(sub < 2, lanes == at).astype(BF16)
            hbuf[h] = jnp.dot(stack.T.astype(BF16), place, preferred_element_type=F32)

    col_lane = lax.broadcasted_iota(jnp.int32, (sections, cb), 1)
    col_row = lax.broadcasted_iota(jnp.int32, (sections, cb), 0)

    def neighbours(a):
        c = tbuf[a + 1]
        up = tbuf[a]
        left = jnp.where(col_lane == 0, 0.0, pltpu.roll(c, 1, 1))
        right = jnp.where(col_lane == cb - 1, 0.0, pltpu.roll(c, cb - 1, 1))
        lap = up + tbuf[a + 2] + (left + right + gather_row(hbuf, a)) - 4.0 * c
        return c, up, lap

    def scatter_row(a, value):
        for h in range(2):
            obuf[h, pl.ds(a, sections, stride=ca), :] = value[:, h * LANES : (h + 1) * LANES]

    stores = [
        pltpu.make_async_copy(
            obuf.at[h], out_hbm.at[0, :, pl.ds(h * LANES, LANES)], out_sem.at[h]
        )
        for h in range(2)
    ]

    @pl.when(g == 0)
    def _():
        owner = owner_ref[...]
        slots = []
        below = lax.broadcasted_iota(jnp.int32, (256, 256), 0)
        after = lax.broadcasted_iota(jnp.int32, (256, 256), 1)
        upto = (below <= after).astype(BF16)
        names = lax.broadcasted_iota(jnp.int32, (owners, 256), 0)
        carry = jnp.zeros((owners, 1), F32)
        for j in range(exit_rows // 256):
            hit = (owner[:, j * 256 : (j + 1) * 256] == names).astype(F32)
            count = jnp.dot(hit.astype(BF16), upto, preferred_element_type=F32) + carry
            slots.append(jnp.sum(hit * (count - 1.0), axis=0, keepdims=True))
            carry = count[:, 255:256]
        slot = jnp.concatenate(slots, axis=1)
        cell = cell_ref[...]
        across = jnp.bitwise_and(cell, cb - 1)
        along = jnp.right_shift(cell, cb.bit_length() - 1)
        par[4:5] = pid_ref[...].astype(F32)
        par[5:6] = along.astype(F32)
        par[6:7] = across.astype(F32)
        par[7:8] = jnp.zeros((1, exit_rows), F32)
        places = lax.broadcasted_iota(jnp.int32, (SLOTS, exit_rows), 0).astype(F32)
        in_slot = (slot == places).astype(BF16)

        finish_halo()

        @pl.loop(0, ca)
        def _(a):
            c, _, lap = neighbours(a)
            back = jnp.where(jnp.bitwise_and(col_row, 7) == 0, 0.0, pltpu.roll(c, 1, 0))
            du = c - back
            layers = sections // 4
            d, m, q, e = (c[v * layers : (v + 1) * layers] for v in range(4))
            dm, dq, de = (du[v * layers : (v + 1) * layers] for v in (1, 2, 3))
            relaxing = relax_rate / (1.0 + d * d)
            fresh = diffusion * lap + jnp.concatenate(
                [
                    d - cfl_nozzle * dm,
                    m - cfl_nozzle * (dm + dq),
                    q + relax_step * relaxing * (e - q) - cfl_nozzle * dq,
                    e - cfl_nozzle * de,
                ],
                axis=0,
            )
            scatter_row(a, fresh)

        for store in stores:
            store.start()

        layers = sections // 4
        halve = jnp.where(
            jnp.right_shift(lax.broadcasted_iota(jnp.int32, (cb, cb // 2), 0), 1)
            == lax.broadcasted_iota(jnp.int32, (cb, cb // 2), 1),
            0.5,
            0.0,
        ).astype(F32)
        halve_rows = jnp.where(
            jnp.right_shift(lax.broadcasted_iota(jnp.int32, (ca // 2, ca), 1), 1)
            == lax.broadcasted_iota(jnp.int32, (ca // 2, ca), 0),
            0.5,
            0.0,
        ).astype(F32)
        coarse = []
        for v in (1, 2, 3):
            at = pl.ds((v * layers + layers - 1) * ca, ca)
            plane = jnp.concatenate([obuf[h, at, :] for h in range(2)], axis=1)
            half = jnp.dot(
                plane, halve, precision=lax.Precision.HIGHEST, preferred_element_type=F32
            )
            coarse.append(
                jnp.dot(
                    halve_rows, half, precision=lax.Precision.HIGHEST, preferred_element_type=F32
                )
            )
        flux, quality, enthalpy = coarse
        strength = jnp.sqrt(1.0 + flux * flux)
        center = (sections - 1) * jax.nn.sigmoid(enthalpy - 2.0 * quality)
        for base, value in ((0, strength), (2, center)):
            hi, lo = split_hi_lo(value)
            for k, part in ((base, hi.astype(F32)), (base + 1, lo.astype(F32))):
                for i in range(ca // 2):
                    par[k : k + 1, i * (cb // 2) : (i + 1) * (cb // 2)] = part[i : i + 1]

        group = 16
        values = par[...]
        tiled = jnp.concatenate([values] * group, axis=0)
        label = jnp.right_shift(lax.broadcasted_iota(jnp.int32, (group * 8, exit_rows), 0), 3)

        @pl.loop(0, owners // group)
        def _(b):
            picked = jnp.where(owner == label + b * group, tiled, 0.0).astype(BF16)
            packed = dot_last(picked, in_slot).reshape(group, 8, SLOTS)
            send_buf[pl.ds(b * group, group)] = jnp.concatenate(
                [packed[:, :, :LANES], packed[:, :, LANES:]], axis=1
            ).astype(BF16)

            @pl.loop(0, group)
            def _(k):
                o = b * group + k
                pltpu.make_async_remote_copy(
                    src_ref=send_buf.at[o],
                    dst_ref=recv_buf.at[me],
                    send_sem=row_send.at[o],
                    recv_sem=row_recv.at[me],
                    device_id=(1, o // n_plane, o % n_plane),
                    device_id_type=MESH,
                ).start()

        @pl.loop(0, owners)
        def _(o):
            pltpu.make_async_remote_copy(
                src_ref=send_buf.at[o],
                dst_ref=recv_buf.at[me],
                send_sem=row_send.at[o],
                recv_sem=row_recv.at[me],
                device_id=(1, o // n_plane, o % n_plane),
                device_id_type=MESH,
            ).wait_send()

    @pl.when(g == 1)
    def _():
        fold_load.wait()
        folded = jnp.dot(coal_ref[...], fold[...], preferred_element_type=F32).astype(BF16)
        evap = jnp.zeros((sections, cb), F32)
        for k in range(sections):
            evap = jnp.where(col_row == k, evap_ref[k], evap)
        speeds = 0.2 + 0.5 * col_row.astype(F32) / (sections - 1)

        finish_halo()

        @pl.loop(0, ca // CHUNK)
        def _(step):
            parts = []
            for t in range(CHUNK):
                c, up, lap = neighbours(step * CHUNK + t)
                lost = evap * c
                gained = jnp.where(
                    col_row == sections - 1, 0.0, pltpu.roll(lost, sections - 1, 0)
                )
                parts.append(c - speeds * (c - up) + diffusion * lap - lost + gained)
            moved = jnp.concatenate(parts, axis=1)
            first = jnp.dot(folded, pair_terms(moved), preferred_element_type=F32)
            middle = moved + (0.5 * collide_step) * first
            second = jnp.dot(folded, pair_terms(middle), preferred_element_type=F32)
            mixed = moved + collide_step * second
            for t in range(CHUNK):
                scatter_row(step * CHUNK + t, mixed[:, t * cb : (t + 1) * cb])

        level = lax.broadcasted_iota(jnp.int32, (sections, SLOTS), 0).astype(F32)
        index_a = lax.broadcasted_iota(jnp.int32, (ca, SLOTS), 0).astype(F32)
        index_b = lax.broadcasted_iota(jnp.int32, (cb, SLOTS), 0).astype(F32)

        @pl.loop(0, owners // SOURCES)
        def _(step):
            lefts, rights = [], []
            for t in range(SOURCES):
                o = step * SOURCES + t
                pltpu.make_async_remote_copy(
                    src_ref=send_buf.at[o],
                    dst_ref=recv_buf.at[o],
                    send_sem=row_send.at[o],
                    recv_sem=row_recv.at[o],
                    device_id=(0, s, p),
                    device_id_type=MESH,
                ).wait_recv()
                block = recv_buf[o].astype(F32)
                got = jnp.concatenate([block[:8], block[8:]], axis=1)
                strength = got[0:1] + got[1:2]
                center = got[2:3] + got[3:4]
                spread = jnp.full((1, SLOTS), width_ref[0], F32)
                for k in range(1, plumes):
                    spread = jnp.where(got[4:5] == float(k), width_ref[k], spread)
                scaled = (level - center) / spread
                weights = 1.0 / (1.0 + scaled * scaled)
                masses = strength * weights / jnp.sum(weights, axis=0, keepdims=True)
                mask = (got[5:6] == index_a).astype(BF16)
                lefts.append(
                    jnp.concatenate(
                        [
                            jnp.broadcast_to(masses[k : k + 1], (ca, SLOTS)).astype(BF16) * mask
                            for k in range(sections)
                        ],
                        axis=0,
                    )
                )
                rights.append((got[6:7] == index_b).astype(BF16))
            left = jnp.concatenate(lefts, axis=1)
            right = jnp.concatenate(rights, axis=1)
            added = dot_last(left, right)
            for h in range(2):
                obuf[h] += added[:, h * LANES : (h + 1) * LANES]

        for store in stores:
            store.start()

    for store in stores:
        store.wait()


def body(n_slab, n_plane, fields, evap_rates, coal_kernel, plume_width, owner_map, deposit_cell, plume_ids):
    _, sections, ca, cb = fields.shape
    exit_rows = owner_map.shape[1]
    owners = n_slab * n_plane
    rows = sections * ca
    fold = jnp.asarray(fold_matrix(sections), BF16)
    kept = fold.shape[1]
    hbm = pl.BlockSpec(memory_space=pl.ANY)
    vmem = pl.BlockSpec(memory_space=pltpu.VMEM)
    smem = pl.BlockSpec(memory_space=pltpu.SMEM)
    out = pl.pallas_call(
        functools.partial(kernel, n_slab, n_plane, sections, ca, cb, exit_rows),
        out_shape=jax.ShapeDtypeStruct((1, rows, cb), F32),
        in_specs=[hbm, smem, vmem, hbm, smem, vmem, vmem, vmem],
        out_specs=hbm,
        scratch_shapes=[
            pltpu.VMEM((2, rows, LANES), F32),
            pltpu.VMEM((ca + 2, sections, cb), F32),
            pltpu.VMEM((2, rows, LANES), F32),
            pltpu.VMEM((2, rows, LANES), F32),
            pltpu.VMEM((sections * sections, kept), BF16),
            pltpu.VMEM((2, 1, rows), F32),
            pltpu.VMEM((2, 1, rows), F32),
            pltpu.VMEM((8, exit_rows), F32),
            pltpu.VMEM((owners, 16, LANES), BF16),
            pltpu.VMEM((owners, 16, LANES), BF16),
            pltpu.SemaphoreType.DMA((2,)),
            pltpu.SemaphoreType.DMA((2,)),
            pltpu.SemaphoreType.DMA,
            pltpu.SemaphoreType.DMA((4,)),
            pltpu.SemaphoreType.DMA((4,)),
            pltpu.SemaphoreType.DMA((owners,)),
            pltpu.SemaphoreType.DMA((owners,)),
        ],
        compiler_params=pltpu.CompilerParams(
            collective_id=0, has_side_effects=True, vmem_limit_bytes=48 * 1024 * 1024
        ),
    )(
        fields.reshape(1, rows, cb), evap_rates, coal_kernel, fold, plume_width,
        owner_map, deposit_cell, plume_ids,
    )
    return out.reshape(1, sections, ca, cb)


def solution(mesh):
    return jax.shard_map(
        functools.partial(body, mesh.shape["slab"], mesh.shape["plane"]),
        mesh=mesh,
        in_specs=(
            P("group", None, "slab", "plane"),
            P(),
            P(),
            P(),
            P(("slab", "plane"), None),
            P(("slab", "plane"), None),
            P(("slab", "plane"), None),
        ),
        out_specs=P("group", None, "slab", "plane"),
        check_vma=False,
    )
```

```python
import functools

import jax
import jax.numpy as jnp
import numpy as np
from jax import lax
from jax.experimental import pallas as pl
from jax.experimental.pallas import tpu as pltpu
from jax.sharding import PartitionSpec as P

MESH = pl.DeviceIdType.MESH
F32 = jnp.float32
BF16 = jnp.bfloat16
LANES = 128
SLOTS = 256
CHUNK = 2
SOURCES = 4
VMEM_BYTES = 63 * 1024 * 1024

cfl_nozzle = 0.35
diffusion = 0.2
relax_rate = 5.0
relax_step = 0.1
collide_step = 0.25


def fold_matrix(sections):
    kept = [(i, j) for i in range(sections) for j in range(i // 8 * 8, sections)]
    fold = np.zeros((sections * sections, len(kept)), np.float32)
    for q, (i, j) in enumerate(kept):
        fold[i * sections + j, q] = 1.0
        if j // 8 > i // 8:
            fold[j * sections + i, q] = 1.0
    return fold


def pair_terms(m):
    sections, width = m.shape
    pieces = []
    for i in range(sections):
        low = i // 8 * 8
        pieces.append(jnp.broadcast_to(m[i : i + 1], (sections - low, width)) * m[low:])
    return jnp.concatenate(pieces, axis=0).astype(BF16)


def split_hi_lo(x):
    hi = x.astype(BF16)
    lo = (x - hi.astype(F32)).astype(BF16)
    return hi, lo


def dot_last(a, b):
    return lax.dot_general(a, b, (((1,), (1,)), ((), ())), preferred_element_type=F32)


def kernel(
    n_slab, n_plane, sections, ca, cb, exit_rows,
    fields_hbm, evap_hbm, coal_hbm, fold_hbm, width_hbm, owner_hbm, cell_hbm, pid_hbm,
    out_hbm,
    fbuf, tbuf, hbuf, obuf, fold, cols_out, cols_in, par, send_buf, recv_buf,
    evap_ref, coal_ref, width_ref, owner_ref, cell_ref, pid_ref,
    in_sem, out_sem, arg_sem, halo_send, halo_recv, row_send, row_recv,
):
    owners = n_slab * n_plane
    plumes = width_ref.shape[0]
    rows = sections * ca
    g = lax.axis_index("group")
    s = lax.axis_index("slab")
    p = lax.axis_index("plane")
    me = s * n_plane + p

    barrier = pltpu.get_barrier_semaphore()
    sides = [
        (s > 0, (g, s - 1, p)),
        (s < n_slab - 1, (g, s + 1, p)),
        (p > 0, (g, s, p - 1)),
        (p < n_plane - 1, (g, s, p + 1)),
    ]
    near = 0
    for there, target in sides:
        near = near + there.astype(jnp.int32)

        @pl.when(there)
        def _():
            pl.semaphore_signal(barrier, inc=1, device_id=target, device_id_type=MESH)

    @pl.when(g == 1)
    def _():
        @pl.loop(0, owners)
        def _(o):
            pl.semaphore_signal(
                barrier, inc=1, device_id=(0, o // n_plane, o % n_plane), device_id_type=MESH
            )

    load = pltpu.make_async_copy(fields_hbm, fbuf, in_sem)
    load.start()
    nozzle_args = [
        pltpu.make_async_copy(source, target, arg_sem.at[k])
        for k, (source, target) in enumerate(
            ((owner_hbm, owner_ref), (cell_hbm, cell_ref), (pid_hbm, pid_ref))
        )
    ]
    spray_args = [
        pltpu.make_async_copy(source, target, arg_sem.at[k])
        for k, (source, target) in enumerate(
            ((evap_hbm, evap_ref), (width_hbm, width_ref), (coal_hbm, coal_ref), (fold_hbm, fold))
        )
    ]

    @pl.when(g == 0)
    def _():
        for copy in nozzle_args:
            copy.start()

    @pl.when(g == 1)
    def _():
        for copy in spray_args:
            copy.start()

    load.wait()

    def lines(a, h):
        return pl.ds(a // 8 * 16 + h * 8 + a % 8, sections, stride=2 * ca)

    def gather_row(ref, a):
        return jnp.concatenate([ref[lines(a, h), :] for h in range(2)], axis=1)

    def half(ref, h):
        return ref[...].reshape(rows // 8, 2, 8, LANES)[:, h].reshape(rows, LANES)

    for a in (0, ca - 1):
        tbuf[a + 1] = gather_row(fbuf, a)

    lane = lax.broadcasted_iota(jnp.int32, (8, LANES), 1)
    for h, at in ((0, 0), (1, LANES - 1)):
        select = (lane == at).astype(BF16)
        hi, lo = split_hi_lo(half(fbuf, h))
        cols_out[h] = (dot_last(select, hi) + dot_last(select, lo))[0:1]

    def halo(kind, target):
        source, landing = (
            (tbuf.at[ca], tbuf.at[0]),
            (tbuf.at[1], tbuf.at[ca + 1]),
            (cols_out.at[1], cols_in.at[0]),
            (cols_out.at[0], cols_in.at[1]),
        )[kind]
        return pltpu.make_async_remote_copy(
            src_ref=source,
            dst_ref=landing,
            send_sem=halo_send.at[kind],
            recv_sem=halo_recv.at[kind],
            device_id=target,
            device_id_type=MESH,
        )

    pl.semaphore_wait(barrier, near + jnp.where(g == 0, owners, 0))

    outgoing = (sides[1], sides[0], sides[3], sides[2])
    for kind in range(4):
        there, target = outgoing[kind]

        @pl.when(there)
        def _():
            halo(kind, target).start()

    @pl.loop(1, ca - 1)
    def _(a):
        tbuf[a + 1] = gather_row(fbuf, a)

    for kind, landing in enumerate((tbuf.at[0], tbuf.at[ca + 1], cols_in.at[0], cols_in.at[1])):

        @pl.when(jnp.logical_not(sides[kind][0]))
        def _():
            landing[...] = jnp.zeros(landing.shape, F32)

    def finish_halo():
        for kind in range(4):

            @pl.when(outgoing[kind][0])
            def _():
                halo(kind, outgoing[kind][1]).wait_send()

            @pl.when(sides[kind][0])
            def _():
                halo(kind, outgoing[kind][1]).wait_recv()

        sub = lax.broadcasted_iota(jnp.int32, (16, LANES), 0)
        lanes = lax.broadcasted_iota(jnp.int32, (16, LANES), 1)
        for h, at in ((0, 0), (1, LANES - 1)):
            hi = cols_in[h].astype(BF16).astype(F32)
            lo = cols_in[h] - hi
            stack = jnp.concatenate([hi, lo, jnp.zeros((14, rows), F32)], axis=0)
            place = jnp.logical_and(sub < 2, lanes == at).astype(BF16)
            placed = jnp.dot(stack.T.astype(BF16), place, preferred_element_type=F32)
            hbuf[h] = placed

    col_lane = lax.broadcasted_iota(jnp.int32, (sections, cb), 1)
    col_row = lax.broadcasted_iota(jnp.int32, (sections, cb), 0)

    def column_halo(a):
        return jnp.concatenate(
            [hbuf[h, pl.ds(a, sections, stride=ca), :] for h in range(2)], axis=1
        )

    def neighbours(a):
        c = tbuf[a + 1]
        up = tbuf[a]
        left = jnp.where(col_lane == 0, 0.0, pltpu.roll(c, 1, 1))
        right = jnp.where(col_lane == cb - 1, 0.0, pltpu.roll(c, cb - 1, 1))
        lap = up + tbuf[a + 2] + (left + right + column_halo(a)) - 4.0 * c
        return c, up, lap

    def scatter_row(a, value):
        for h in range(2):
            obuf[lines(a, h), :] = value[:, h * LANES : (h + 1) * LANES]

    store = pltpu.make_async_copy(obuf, out_hbm, out_sem)

    @pl.when(g == 0)
    def _():
        for copy in nozzle_args:
            copy.wait()
        owner = owner_ref[...]
        slots = []
        below = lax.broadcasted_iota(jnp.int32, (256, 256), 0)
        after = lax.broadcasted_iota(jnp.int32, (256, 256), 1)
        upto = (below <= after).astype(BF16)
        names = lax.broadcasted_iota(jnp.int32, (owners, 256), 0)
        carry = jnp.zeros((owners, 1), F32)
        for j in range(exit_rows // 256):
            hit = (owner[:, j * 256 : (j + 1) * 256] == names).astype(F32)
            count = jnp.dot(hit.astype(BF16), upto, preferred_element_type=F32) + carry
            slots.append(jnp.sum(hit * (count - 1.0), axis=0, keepdims=True))
            carry = count[:, 255:256]
        slot = jnp.concatenate(slots, axis=1)
        cell = cell_ref[...]
        across = jnp.bitwise_and(cell, cb - 1)
        along = jnp.right_shift(cell, cb.bit_length() - 1)
        par[4:5] = pid_ref[...].astype(F32)
        par[5:6] = along.astype(F32)
        par[6:7] = across.astype(F32)
        par[7:8] = jnp.zeros((1, exit_rows), F32)
        places = lax.broadcasted_iota(jnp.int32, (SLOTS, exit_rows), 0).astype(F32)
        in_slot = (slot == places).astype(BF16)

        finish_halo()

        @pl.loop(0, ca)
        def _(a):
            c, _, lap = neighbours(a)
            back = jnp.where(jnp.bitwise_and(col_row, 7) == 0, 0.0, pltpu.roll(c, 1, 0))
            du = c - back
            layers = sections // 4
            d, m, q, e = (c[v * layers : (v + 1) * layers] for v in range(4))
            dm, dq, de = (du[v * layers : (v + 1) * layers] for v in (1, 2, 3))
            relaxing = relax_rate / (1.0 + d * d)
            fresh = diffusion * lap + jnp.concatenate(
                [
                    d - cfl_nozzle * dm,
                    m - cfl_nozzle * (dm + dq),
                    q + relax_step * relaxing * (e - q) - cfl_nozzle * dq,
                    e - cfl_nozzle * de,
                ],
                axis=0,
            )
            scatter_row(a, fresh)

        store.start()

        layers = sections // 4
        halve = jnp.where(
            jnp.right_shift(lax.broadcasted_iota(jnp.int32, (cb, cb // 2), 0), 1)
            == lax.broadcasted_iota(jnp.int32, (cb, cb // 2), 1),
            0.5,
            0.0,
        ).astype(F32)
        halve_rows = jnp.where(
            jnp.right_shift(lax.broadcasted_iota(jnp.int32, (ca // 2, ca), 1), 1)
            == lax.broadcasted_iota(jnp.int32, (ca // 2, ca), 0),
            0.5,
            0.0,
        ).astype(F32)
        coarse = []
        for v in (1, 2, 3):
            at = pl.ds((v * layers + layers - 1) * 2 * ca, 2 * ca)
            tiles = obuf[at, :].reshape(ca // 8, 2, 8, LANES)
            plane = jnp.concatenate([tiles[:, h].reshape(ca, LANES) for h in range(2)], axis=1)
            across_mean = jnp.dot(
                plane, halve, precision=lax.Precision.HIGHEST, preferred_element_type=F32
            )
            coarse.append(
                jnp.dot(
                    halve_rows, across_mean, precision=lax.Precision.HIGHEST, preferred_element_type=F32
                )
            )
        flux, quality, enthalpy = coarse
        strength = jnp.sqrt(1.0 + flux * flux)
        center = (sections - 1) * jax.nn.sigmoid(enthalpy - 2.0 * quality)
        for base, value in ((0, strength), (2, center)):
            hi, lo = split_hi_lo(value)
            for k, part in ((base, hi.astype(F32)), (base + 1, lo.astype(F32))):
                for i in range(ca // 2):
                    par[k : k + 1, i * (cb // 2) : (i + 1) * (cb // 2)] = part[i : i + 1]

        group = 16
        values = par[...]
        tiled = jnp.concatenate([values] * group, axis=0)
        label = jnp.right_shift(lax.broadcasted_iota(jnp.int32, (group * 8, exit_rows), 0), 3)

        @pl.loop(0, owners // group)
        def _(b):
            picked = jnp.where(owner == label + b * group, tiled, 0.0).astype(BF16)
            packed = dot_last(picked, in_slot).reshape(group, 8, SLOTS)
            send_buf[pl.ds(b * group, group)] = jnp.concatenate(
                [packed[:, :, :LANES], packed[:, :, LANES:]], axis=1
            ).astype(BF16)

            @pl.loop(0, group)
            def _(k):
                o = b * group + k
                pltpu.make_async_remote_copy(
                    src_ref=send_buf.at[o],
                    dst_ref=recv_buf.at[me],
                    send_sem=row_send.at[o],
                    recv_sem=row_recv.at[me],
                    device_id=(1, o // n_plane, o % n_plane),
                    device_id_type=MESH,
                ).start()

        @pl.loop(0, owners)
        def _(o):
            pltpu.make_async_remote_copy(
                src_ref=send_buf.at[o],
                dst_ref=recv_buf.at[me],
                send_sem=row_send.at[o],
                recv_sem=row_recv.at[me],
                device_id=(1, o // n_plane, o % n_plane),
                device_id_type=MESH,
            ).wait_send()

    @pl.when(g == 1)
    def _():
        for copy in spray_args:
            copy.wait()
        folded = jnp.dot(coal_ref[...], fold[...], preferred_element_type=F32).astype(BF16)
        evap = jnp.zeros((sections, cb), F32)
        for k in range(sections):
            evap = jnp.where(col_row == k, evap_ref[k], evap)
        speeds = 0.2 + 0.5 * col_row.astype(F32) / (sections - 1)

        finish_halo()

        @pl.loop(0, ca // CHUNK)
        def _(step):
            parts = []
            for t in range(CHUNK):
                c, up, lap = neighbours(step * CHUNK + t)
                lost = evap * c
                gained = jnp.where(
                    col_row == sections - 1, 0.0, pltpu.roll(lost, sections - 1, 0)
                )
                parts.append(c - speeds * (c - up) + diffusion * lap - lost + gained)
            moved = jnp.concatenate(parts, axis=1)
            first = jnp.dot(folded, pair_terms(moved), preferred_element_type=F32)
            middle = moved + (0.5 * collide_step) * first
            second = jnp.dot(folded, pair_terms(middle), preferred_element_type=F32)
            mixed = moved + collide_step * second
            for t in range(CHUNK):
                scatter_row(step * CHUNK + t, mixed[:, t * cb : (t + 1) * cb])

        level = lax.broadcasted_iota(jnp.int32, (sections, SLOTS), 0).astype(F32)
        index_a = lax.broadcasted_iota(jnp.int32, (ca, SLOTS), 0).astype(F32)
        index_b = lax.broadcasted_iota(jnp.int32, (cb, SLOTS), 0).astype(F32)

        @pl.loop(0, owners // SOURCES)
        def _(step):
            lefts, rights = [], []
            for t in range(SOURCES):
                o = step * SOURCES + t
                pltpu.make_async_remote_copy(
                    src_ref=send_buf.at[o],
                    dst_ref=recv_buf.at[o],
                    send_sem=row_send.at[o],
                    recv_sem=row_recv.at[o],
                    device_id=(0, s, p),
                    device_id_type=MESH,
                ).wait_recv()
                block = recv_buf[o].astype(F32)
                got = jnp.concatenate([block[:8], block[8:]], axis=1)
                strength = got[0:1] + got[1:2]
                center = got[2:3] + got[3:4]
                spread = jnp.full((1, SLOTS), width_ref[0], F32)
                for k in range(1, plumes):
                    spread = jnp.where(got[4:5] == float(k), width_ref[k], spread)
                scaled = (level - center) / spread
                weights = 1.0 / (1.0 + scaled * scaled)
                masses = strength * weights / jnp.sum(weights, axis=0, keepdims=True)
                mask = (got[5:6] == index_a).astype(BF16)
                lefts.append(
                    jnp.concatenate(
                        [
                            jnp.broadcast_to(masses[k : k + 1], (ca, SLOTS)).astype(BF16) * mask
                            for k in range(sections)
                        ],
                        axis=0,
                    )
                )
                rights.append((got[6:7] == index_b).astype(BF16))
            left = jnp.concatenate(lefts, axis=1)
            right = jnp.concatenate(rights, axis=1)
            added = dot_last(left, right)
            tiles = jnp.stack(
                [added[:, h * LANES : (h + 1) * LANES].reshape(rows // 8, 8, LANES) for h in range(2)],
                axis=1,
            )
            obuf[...] += tiles.reshape(2 * rows, LANES)

        store.start()

    store.wait()


def body(n_slab, n_plane, fields, evap_rates, coal_kernel, plume_width, owner_map, deposit_cell, plume_ids):
    _, sections, ca, cb = fields.shape
    exit_rows = owner_map.shape[1]
    owners = n_slab * n_plane
    rows = sections * ca
    fold = jnp.asarray(fold_matrix(sections), BF16)
    kept = fold.shape[1]
    hbm = pl.BlockSpec(memory_space=pl.ANY)
    out = pl.pallas_call(
        functools.partial(kernel, n_slab, n_plane, sections, ca, cb, exit_rows),
        out_shape=jax.ShapeDtypeStruct((2 * rows, LANES), F32),
        in_specs=[hbm] * 8,
        out_specs=hbm,
        scratch_shapes=[
            pltpu.VMEM((2 * rows, LANES), F32),
            pltpu.VMEM((ca + 2, sections, cb), F32),
            pltpu.VMEM((2, rows, LANES), F32),
            pltpu.VMEM((2 * rows, LANES), F32),
            pltpu.VMEM((sections * sections, kept), BF16),
            pltpu.VMEM((2, 1, rows), F32),
            pltpu.VMEM((2, 1, rows), F32),
            pltpu.VMEM((8, exit_rows), F32),
            pltpu.VMEM((owners, 16, LANES), BF16),
            pltpu.VMEM((owners, 16, LANES), BF16),
            pltpu.SMEM(evap_rates.shape, F32),
            pltpu.VMEM(coal_kernel.shape, BF16),
            pltpu.SMEM(plume_width.shape, F32),
            pltpu.VMEM((1, exit_rows), jnp.int32),
            pltpu.VMEM((1, exit_rows), jnp.int32),
            pltpu.VMEM((1, exit_rows), jnp.int32),
            pltpu.SemaphoreType.DMA,
            pltpu.SemaphoreType.DMA,
            pltpu.SemaphoreType.DMA((4,)),
            pltpu.SemaphoreType.DMA((4,)),
            pltpu.SemaphoreType.DMA((4,)),
            pltpu.SemaphoreType.DMA((owners,)),
            pltpu.SemaphoreType.DMA((owners,)),
        ],
        compiler_params=pltpu.CompilerParams(
            collective_id=0, has_side_effects=True, vmem_limit_bytes=VMEM_BYTES
        ),
    )(
        fields.reshape(rows // 8, 8, 2, LANES).transpose(0, 2, 1, 3).reshape(2 * rows, LANES), evap_rates, coal_kernel, fold, plume_width,
        owner_map, deposit_cell, plume_ids,
    )
    out = out.reshape(rows // 8, 2, 8, LANES).transpose(0, 2, 1, 3)
    return out.reshape(1, sections, ca, cb)


def solution(mesh):
    return jax.shard_map(
        functools.partial(body, mesh.shape["slab"], mesh.shape["plane"]),
        mesh=mesh,
        in_specs=(
            P("group", None, "slab", "plane"),
            P(),
            P(),
            P(),
            P(("slab", "plane"), None),
            P(("slab", "plane"), None),
            P(("slab", "plane"), None),
        ),
        out_specs=P("group", None, "slab", "plane"),
        check_vma=False,
    )
```

```python
import functools

import jax
import jax.numpy as jnp
import numpy as np
from jax import lax
from jax.experimental import pallas as pl
from jax.experimental.pallas import tpu as pltpu
from jax.sharding import PartitionSpec as P

MESH = pl.DeviceIdType.MESH
F32 = jnp.float32
BF16 = jnp.bfloat16
LANES = 128
SLOTS = 256
CHUNK = 4
SOURCES = 4
VMEM_BYTES = 63 * 1024 * 1024

cfl_nozzle = 0.35
diffusion = 0.2
relax_rate = 5.0
relax_step = 0.1
collide_step = 0.25


def fold_matrix(sections):
    kept = [(i, j) for i in range(sections) for j in range(i // 8 * 8, sections)]
    fold = np.zeros((sections * sections, len(kept)), np.float32)
    for q, (i, j) in enumerate(kept):
        fold[i * sections + j, q] = 1.0
        if j // 8 > i // 8:
            fold[j * sections + i, q] = 1.0
    return fold


def pair_terms(m):
    sections, width = m.shape
    pieces = []
    for i in range(sections):
        low = i // 8 * 8
        pieces.append(jnp.broadcast_to(m[i : i + 1], (sections - low, width)) * m[low:])
    return jnp.concatenate(pieces, axis=0).astype(BF16)


def split_hi_lo(x):
    hi = x.astype(BF16)
    lo = (x - hi.astype(F32)).astype(BF16)
    return hi, lo


def dot_last(a, b):
    return lax.dot_general(a, b, (((1,), (1,)), ((), ())), preferred_element_type=F32)


def kernel(
    n_slab, n_plane, sections, ca, cb, exit_rows,
    fields_hbm, evap_hbm, coal_hbm, fold_hbm, width_hbm, owner_hbm, cell_hbm, pid_hbm,
    out_hbm,
    fbuf, tbuf, hbuf, obuf, fold, cols_out, cols_in, par, send_buf, recv_buf,
    evap_ref, coal_ref, width_ref, owner_ref, cell_ref, pid_ref, picks, in_slot,
    in_sem, out_sem, arg_sem, halo_send, halo_recv, row_send, row_recv,
):
    owners = n_slab * n_plane
    plumes = width_ref.shape[0]
    rows = sections * ca
    g = lax.axis_index("group")
    s = lax.axis_index("slab")
    p = lax.axis_index("plane")
    me = s * n_plane + p

    barrier = pltpu.get_barrier_semaphore()
    sides = [
        (s > 0, (g, s - 1, p)),
        (s < n_slab - 1, (g, s + 1, p)),
        (p > 0, (g, s, p - 1)),
        (p < n_plane - 1, (g, s, p + 1)),
    ]
    near = 0
    for there, target in sides:
        near = near + there.astype(jnp.int32)

        @pl.when(there)
        def _():
            pl.semaphore_signal(barrier, inc=1, device_id=target, device_id_type=MESH)

    @pl.when(g == 1)
    def _():
        @pl.loop(0, owners)
        def _(o):
            pl.semaphore_signal(
                barrier, inc=1, device_id=(0, o // n_plane, o % n_plane), device_id_type=MESH
            )

    load = pltpu.make_async_copy(fields_hbm, fbuf, in_sem)
    load.start()
    nozzle_args = [
        pltpu.make_async_copy(source, target, arg_sem.at[k])
        for k, (source, target) in enumerate(
            ((owner_hbm, owner_ref), (cell_hbm, cell_ref), (pid_hbm, pid_ref))
        )
    ]
    spray_args = [
        pltpu.make_async_copy(source, target, arg_sem.at[k])
        for k, (source, target) in enumerate(
            ((evap_hbm, evap_ref), (width_hbm, width_ref), (coal_hbm, coal_ref), (fold_hbm, fold))
        )
    ]

    @pl.when(g == 0)
    def _():
        for copy in nozzle_args:
            copy.start()

    @pl.when(g == 1)
    def _():
        for copy in spray_args:
            copy.start()

    load.wait()

    def lines(a, h):
        return pl.ds(a // 8 * 16 + h * 8 + a % 8, sections, stride=2 * ca)

    def gather_row(ref, a):
        return jnp.concatenate([ref[lines(a, h), :] for h in range(2)], axis=1)

    def half(ref, h):
        return ref[...].reshape(rows // 8, 2, 8, LANES)[:, h].reshape(rows, LANES)

    for a in (0, ca - 1):
        tbuf[a + 1] = gather_row(fbuf, a)

    def halo(kind, target):
        source, landing = (
            (tbuf.at[ca], tbuf.at[0]),
            (tbuf.at[1], tbuf.at[ca + 1]),
            (cols_out.at[1], cols_in.at[0]),
            (cols_out.at[0], cols_in.at[1]),
        )[kind]
        return pltpu.make_async_remote_copy(
            src_ref=source,
            dst_ref=landing,
            send_sem=halo_send.at[kind],
            recv_sem=halo_recv.at[kind],
            device_id=target,
            device_id_type=MESH,
        )

    pl.semaphore_wait(barrier, near + jnp.where(g == 0, owners, 0))

    outgoing = (sides[1], sides[0], sides[3], sides[2])
    def start_halo(kinds):
        for kind in kinds:

            @pl.when(outgoing[kind][0])
            def _():
                halo(kind, outgoing[kind][1]).start()

    start_halo((0, 1))

    lane = lax.broadcasted_iota(jnp.int32, (8, LANES), 1)
    for h, at in ((0, 0), (1, LANES - 1)):
        select = (lane == at).astype(BF16)
        cols_out[h] = dot_last(select, half(fbuf, h).astype(BF16))[0:1]

    start_halo((2, 3))

    @pl.loop(1, ca - 1)
    def _(a):
        tbuf[a + 1] = gather_row(fbuf, a)

    for kind, landing in enumerate((tbuf.at[0], tbuf.at[ca + 1], cols_in.at[0], cols_in.at[1])):

        @pl.when(jnp.logical_not(sides[kind][0]))
        def _():
            landing[...] = jnp.zeros(landing.shape, F32)

    def finish_halo():
        for kind in range(4):

            @pl.when(outgoing[kind][0])
            def _():
                halo(kind, outgoing[kind][1]).wait_send()

            @pl.when(sides[kind][0])
            def _():
                halo(kind, outgoing[kind][1]).wait_recv()

        sub = lax.broadcasted_iota(jnp.int32, (16, cb), 0)
        lanes = lax.broadcasted_iota(jnp.int32, (16, cb), 1)
        stack = jnp.concatenate([cols_in[0], cols_in[1], jnp.zeros((14, rows), F32)], axis=0)
        place = jnp.logical_or(
            jnp.logical_and(sub == 0, lanes == 0), jnp.logical_and(sub == 1, lanes == cb - 1)
        ).astype(BF16)
        placed = jnp.dot(stack.T.astype(BF16), place, preferred_element_type=F32)
        for h in range(2):
            hbuf[h] = placed[:, h * LANES : (h + 1) * LANES]

    col_lane = lax.broadcasted_iota(jnp.int32, (sections, cb), 1)
    col_row = lax.broadcasted_iota(jnp.int32, (sections, cb), 0)

    def column_halo(a):
        return jnp.concatenate(
            [hbuf[h, pl.ds(a, sections, stride=ca), :] for h in range(2)], axis=1
        )

    def neighbours(a):
        c = tbuf[a + 1]
        up = tbuf[a]
        left = jnp.where(col_lane == 0, 0.0, pltpu.roll(c, 1, 1))
        right = jnp.where(col_lane == cb - 1, 0.0, pltpu.roll(c, cb - 1, 1))
        lap = up + tbuf[a + 2] + (left + right + column_halo(a)) - 4.0 * c
        return c, up, lap

    def scatter_row(a, value):
        for h in range(2):
            obuf[lines(a, h), :] = value[:, h * LANES : (h + 1) * LANES]

    store = pltpu.make_async_copy(obuf, out_hbm, out_sem)

    @pl.when(g == 0)
    def _():
        for copy in nozzle_args:
            copy.wait()
        owner = owner_ref[...]
        slots = []
        below = lax.broadcasted_iota(jnp.int32, (256, 256), 0)
        after = lax.broadcasted_iota(jnp.int32, (256, 256), 1)
        upto = (below <= after).astype(BF16)
        names = lax.broadcasted_iota(jnp.int32, (owners, 256), 0)
        carry = jnp.zeros((owners, 1), F32)
        for j in range(exit_rows // 256):
            hit = (owner[:, j * 256 : (j + 1) * 256] == names).astype(F32)
            count = jnp.dot(hit.astype(BF16), upto, preferred_element_type=F32) + carry
            slots.append(jnp.sum(hit * (count - 1.0), axis=0, keepdims=True))
            carry = count[:, 255:256]
        slot = jnp.concatenate(slots, axis=1)
        cell = cell_ref[...]
        across = jnp.bitwise_and(cell, cb - 1)
        along = jnp.right_shift(cell, cb.bit_length() - 1)
        par[4:5] = pid_ref[...].astype(F32)
        par[5:6] = along.astype(F32)
        par[6:7] = across.astype(F32)
        par[7:8] = jnp.zeros((1, exit_rows), F32)
        places = lax.broadcasted_iota(jnp.int32, (SLOTS, exit_rows), 0).astype(F32)
        in_slot[...] = (slot == places).astype(BF16)
        group = 16
        label = jnp.right_shift(lax.broadcasted_iota(jnp.int32, (group * 8, exit_rows), 0), 3)

        @pl.loop(0, owners // group)
        def _(b):
            picks[pl.ds(pl.multiple_of(b * group * 8, group * 8), group * 8)] = (
                owner == label + b * group
            ).astype(BF16)

        halve = jnp.where(
            jnp.right_shift(lax.broadcasted_iota(jnp.int32, (cb, cb // 2), 0), 1)
            == lax.broadcasted_iota(jnp.int32, (cb, cb // 2), 1),
            0.25,
            0.0,
        ).astype(BF16)

        finish_halo()

        layers = sections // 4
        plane_row = lax.broadcasted_iota(jnp.int32, (ca, cb), 0)
        plane_lane = lax.broadcasted_iota(jnp.int32, (ca, cb), 1)

        def plane(k):
            tiles = fbuf[pl.ds(k * 2 * ca, 2 * ca), :].reshape(ca // 8, 2, 8, LANES)
            return jnp.concatenate([tiles[:, h].reshape(ca, LANES) for h in range(2)], axis=1)

        def plane_lap(c, k):
            up = jnp.where(plane_row == 0, tbuf[0, k : k + 1], pltpu.roll(c, 1, 0))
            down = jnp.where(
                plane_row == ca - 1, tbuf[ca + 1, k : k + 1], pltpu.roll(c, ca - 1, 0)
            )
            left = jnp.where(plane_lane == 0, 0.0, pltpu.roll(c, 1, 1))
            right = jnp.where(plane_lane == cb - 1, 0.0, pltpu.roll(c, cb - 1, 1))
            at = pl.ds(k * ca, ca)
            halo_col = jnp.concatenate([hbuf[h, at] for h in range(2)], axis=1)
            return up + down + (left + right + halo_col) - 4.0 * c

        last = [v * layers + layers - 1 for v in range(4)]
        d, m, q, e = (plane(k) for k in last)
        if layers > 1:
            dm, dq, de = (x - plane(k - 1) for x, k in zip((m, q, e), last[1:]))
        else:
            dm, dq, de = m, q, e
        relaxing = relax_rate / (1.0 + d * d)
        exits = [
            m - cfl_nozzle * (dm + dq) + diffusion * plane_lap(m, last[1]),
            q
            + relax_step * relaxing * (e - q)
            - cfl_nozzle * dq
            + diffusion * plane_lap(q, last[2]),
            e - cfl_nozzle * de + diffusion * plane_lap(e, last[3]),
        ]
        paired = jnp.concatenate([x + pltpu.roll(x, ca - 1, 0) for x in exits], axis=0)
        hi = paired.astype(BF16)
        rest = paired - hi.astype(F32)
        mid, low = split_hi_lo(rest)
        sums = jnp.dot(
            jnp.concatenate([hi, mid, low], axis=0), halve, preferred_element_type=F32
        )
        coarse = sums[: 3 * ca] + sums[3 * ca : 6 * ca] + sums[6 * ca :]
        flux, quality, enthalpy = (coarse[v * ca : (v + 1) * ca] for v in range(3))
        strength = jnp.sqrt(1.0 + flux * flux)
        center = (sections - 1) * jax.nn.sigmoid(enthalpy - 2.0 * quality)
        for base, value in ((0, strength), (2, center)):
            hi, low = split_hi_lo(value)
            for k, part in ((base, hi.astype(F32)), (base + 1, low.astype(F32))):
                for i in range(ca // 2):
                    par[k : k + 1, i * (cb // 2) : (i + 1) * (cb // 2)] = part[2 * i : 2 * i + 1]

        values = par[...].astype(BF16)
        tiled = jnp.concatenate([values] * group, axis=0)

        @pl.loop(0, owners // group)
        def _(b):
            picked = tiled * picks[pl.ds(pl.multiple_of(b * group * 8, group * 8), group * 8)]
            packed = dot_last(picked, in_slot[...]).reshape(group, 8, SLOTS)
            send_buf[pl.ds(b * group, group)] = jnp.concatenate(
                [packed[:, :, :LANES], packed[:, :, LANES:]], axis=1
            ).astype(BF16)

            @pl.loop(0, group)
            def _(k):
                o = b * group + k
                pltpu.make_async_remote_copy(
                    src_ref=send_buf.at[o],
                    dst_ref=recv_buf.at[me],
                    send_sem=row_send.at[o],
                    recv_sem=row_recv.at[me],
                    device_id=(1, o // n_plane, o % n_plane),
                    device_id_type=MESH,
                ).start()

        @pl.loop(0, ca // CHUNK)
        def _(step):
            for t in range(CHUNK):
                a = step * CHUNK + t
                c, _, lap = neighbours(a)
                back = jnp.where(jnp.bitwise_and(col_row, layers - 1) == 0, 0.0, pltpu.roll(c, 1, 0))
                du = c - back
                d, m, q, e = (c[v * layers : (v + 1) * layers] for v in range(4))
                dm, dq, de = (du[v * layers : (v + 1) * layers] for v in (1, 2, 3))
                relaxing = relax_rate / (1.0 + d * d)
                fresh = diffusion * lap + jnp.concatenate(
                    [
                        d - cfl_nozzle * dm,
                        m - cfl_nozzle * (dm + dq),
                        q + relax_step * relaxing * (e - q) - cfl_nozzle * dq,
                        e - cfl_nozzle * de,
                    ],
                    axis=0,
                )
                scatter_row(a, fresh)

        store.start()

        @pl.loop(0, owners)
        def _(o):
            pltpu.make_async_remote_copy(
                src_ref=send_buf.at[o],
                dst_ref=recv_buf.at[me],
                send_sem=row_send.at[o],
                recv_sem=row_recv.at[me],
                device_id=(1, o // n_plane, o % n_plane),
                device_id_type=MESH,
            ).wait_send()

    @pl.when(g == 1)
    def _():
        for copy in spray_args:
            copy.wait()
        folded = jnp.dot(coal_ref[...], fold[...], preferred_element_type=F32).astype(BF16)
        evap = jnp.zeros((sections, cb), F32)
        for k in range(sections):
            evap = jnp.where(col_row == k, evap_ref[k], evap)
        speeds = 0.2 + 0.5 * col_row.astype(F32) / (sections - 1)

        finish_halo()

        @pl.loop(0, ca // CHUNK)
        def _(step):
            parts = []
            for t in range(CHUNK):
                c, up, lap = neighbours(step * CHUNK + t)
                lost = evap * c
                gained = jnp.where(
                    col_row == sections - 1, 0.0, pltpu.roll(lost, sections - 1, 0)
                )
                parts.append(c - speeds * (c - up) + diffusion * lap - lost + gained)
            moved = jnp.concatenate(parts, axis=1)
            first = jnp.dot(folded, pair_terms(moved), preferred_element_type=F32)
            middle = moved + (0.5 * collide_step) * first
            second = jnp.dot(folded, pair_terms(middle), preferred_element_type=F32)
            mixed = moved + collide_step * second
            for t in range(CHUNK):
                scatter_row(step * CHUNK + t, mixed[:, t * cb : (t + 1) * cb])

        level = lax.broadcasted_iota(jnp.int32, (sections, SLOTS), 0).astype(F32)
        index_a = lax.broadcasted_iota(jnp.int32, (ca, SLOTS), 0).astype(F32)
        index_b = lax.broadcasted_iota(jnp.int32, (cb, SLOTS), 0).astype(F32)

        @pl.loop(0, owners // SOURCES)
        def _(step):
            lefts, rights = [], []
            for t in range(SOURCES):
                o = step * SOURCES + t
                pltpu.make_async_remote_copy(
                    src_ref=send_buf.at[o],
                    dst_ref=recv_buf.at[o],
                    send_sem=row_send.at[o],
                    recv_sem=row_recv.at[o],
                    device_id=(0, s, p),
                    device_id_type=MESH,
                ).wait_recv()
                block = recv_buf[o].astype(F32)
                got = jnp.concatenate([block[:8], block[8:]], axis=1)
                strength = got[0:1] + got[1:2]
                center = got[2:3] + got[3:4]
                spread = jnp.full((1, SLOTS), width_ref[0], F32)
                for k in range(1, plumes):
                    spread = jnp.where(got[4:5] == float(k), width_ref[k], spread)
                scaled = (level - center) / spread
                weights = 1.0 / (1.0 + scaled * scaled)
                masses = strength * weights / jnp.sum(weights, axis=0, keepdims=True)
                mask = (got[5:6] == index_a).astype(BF16)
                lefts.append(
                    jnp.concatenate(
                        [
                            jnp.broadcast_to(masses[k : k + 1], (ca, SLOTS)).astype(BF16) * mask
                            for k in range(sections)
                        ],
                        axis=0,
                    )
                )
                rights.append((got[6:7] == index_b).astype(BF16))
            left = jnp.concatenate(lefts, axis=1)
            right = jnp.concatenate(rights, axis=1)
            added = dot_last(left, right)
            tiles = jnp.stack(
                [added[:, h * LANES : (h + 1) * LANES].reshape(rows // 8, 8, LANES) for h in range(2)],
                axis=1,
            )
            obuf[...] += tiles.reshape(2 * rows, LANES)

        store.start()

    store.wait()


def body(n_slab, n_plane, fields, evap_rates, coal_kernel, plume_width, owner_map, deposit_cell, plume_ids):
    _, sections, ca, cb = fields.shape
    exit_rows = owner_map.shape[1]
    owners = n_slab * n_plane
    rows = sections * ca
    fold = jnp.asarray(fold_matrix(sections), BF16)
    kept = fold.shape[1]
    hbm = pl.BlockSpec(memory_space=pl.ANY)
    out = pl.pallas_call(
        functools.partial(kernel, n_slab, n_plane, sections, ca, cb, exit_rows),
        out_shape=jax.ShapeDtypeStruct((2 * rows, LANES), F32),
        in_specs=[hbm] * 8,
        out_specs=hbm,
        scratch_shapes=[
            pltpu.VMEM((2 * rows, LANES), F32),
            pltpu.VMEM((ca + 2, sections, cb), F32),
            pltpu.VMEM((2, rows, LANES), F32),
            pltpu.VMEM((2 * rows, LANES), F32),
            pltpu.VMEM((sections * sections, kept), BF16),
            pltpu.VMEM((2, 1, rows), F32),
            pltpu.VMEM((2, 1, rows), F32),
            pltpu.VMEM((8, exit_rows), F32),
            pltpu.VMEM((owners, 16, LANES), BF16),
            pltpu.VMEM((owners, 16, LANES), BF16),
            pltpu.SMEM(evap_rates.shape, F32),
            pltpu.VMEM(coal_kernel.shape, BF16),
            pltpu.SMEM(plume_width.shape, F32),
            pltpu.VMEM((1, exit_rows), jnp.int32),
            pltpu.VMEM((1, exit_rows), jnp.int32),
            pltpu.VMEM((1, exit_rows), jnp.int32),
            pltpu.VMEM((owners * 8, exit_rows), BF16),
            pltpu.VMEM((SLOTS, exit_rows), BF16),
            pltpu.SemaphoreType.DMA,
            pltpu.SemaphoreType.DMA,
            pltpu.SemaphoreType.DMA((4,)),
            pltpu.SemaphoreType.DMA((4,)),
            pltpu.SemaphoreType.DMA((4,)),
            pltpu.SemaphoreType.DMA((owners,)),
            pltpu.SemaphoreType.DMA((owners,)),
        ],
        compiler_params=pltpu.CompilerParams(
            collective_id=0, has_side_effects=True, vmem_limit_bytes=VMEM_BYTES
        ),
    )(
        fields.reshape(rows // 8, 8, 2, LANES).transpose(0, 2, 1, 3).reshape(2 * rows, LANES), evap_rates, coal_kernel, fold, plume_width,
        owner_map, deposit_cell, plume_ids,
    )
    out = out.reshape(rows // 8, 2, 8, LANES).transpose(0, 2, 1, 3)
    return out.reshape(1, sections, ca, cb)


def solution(mesh):
    return jax.shard_map(
        functools.partial(body, mesh.shape["slab"], mesh.shape["plane"]),
        mesh=mesh,
        in_specs=(
            P("group", None, "slab", "plane"),
            P(),
            P(),
            P(),
            P(("slab", "plane"), None),
            P(("slab", "plane"), None),
            P(("slab", "plane"), None),
        ),
        out_specs=P("group", None, "slab", "plane"),
        check_vma=False,
    )
```

```python
import functools

import jax
import jax.numpy as jnp
import numpy as np
from jax import lax
from jax.experimental import pallas as pl
from jax.experimental.pallas import tpu as pltpu
from jax.sharding import PartitionSpec as P

MESH = pl.DeviceIdType.MESH
F32 = jnp.float32
BF16 = jnp.bfloat16
LANES = 128
SLOTS = 256
CHUNK = 4
SOURCES = 4
VMEM_BYTES = 63 * 1024 * 1024

cfl_nozzle = 0.35
diffusion = 0.2
relax_rate = 5.0
relax_step = 0.1
collide_step = 0.25


def fold_matrix(sections):
    kept = [(i, j) for i in range(sections) for j in range(i // 8 * 8, sections)]
    fold = np.zeros((sections * sections, len(kept)), np.float32)
    for q, (i, j) in enumerate(kept):
        fold[i * sections + j, q] = 1.0
        if j // 8 > i // 8:
            fold[j * sections + i, q] = 1.0
    return fold


def pair_terms(m):
    sections, width = m.shape
    pieces = []
    for i in range(sections):
        low = i // 8 * 8
        pieces.append(jnp.broadcast_to(m[i : i + 1], (sections - low, width)) * m[low:])
    return jnp.concatenate(pieces, axis=0).astype(BF16)


def split_hi_lo(x):
    hi = x.astype(BF16)
    lo = (x - hi.astype(F32)).astype(BF16)
    return hi, lo


def dot_last(a, b):
    return lax.dot_general(a, b, (((1,), (1,)), ((), ())), preferred_element_type=F32)


def kernel(
    n_slab, n_plane, sections, ca, cb, exit_rows,
    fields_hbm, evap_hbm, coal_hbm, fold_hbm, width_hbm, owner_hbm, cell_hbm, pid_hbm,
    out_hbm,
    fbuf, tbuf, hbuf, obuf, fold, cols_out, cols_in, par, send_buf, recv_buf,
    evap_ref, coal_ref, width_ref, owner_ref, cell_ref, pid_ref, picks, in_slot,
    in_sem, out_sem, arg_sem, halo_send, halo_recv, row_send, row_recv,
):
    owners = n_slab * n_plane
    plumes = width_ref.shape[0]
    rows = sections * ca
    g = lax.axis_index("group")
    s = lax.axis_index("slab")
    p = lax.axis_index("plane")
    me = s * n_plane + p

    load = pltpu.make_async_copy(fields_hbm, fbuf, in_sem)
    load.start()
    nozzle_args = [
        pltpu.make_async_copy(source, target, arg_sem.at[k])
        for k, (source, target) in enumerate(
            ((owner_hbm, owner_ref), (cell_hbm, cell_ref), (pid_hbm, pid_ref))
        )
    ]
    spray_args = [
        pltpu.make_async_copy(source, target, arg_sem.at[k])
        for k, (source, target) in enumerate(
            ((evap_hbm, evap_ref), (width_hbm, width_ref), (coal_hbm, coal_ref), (fold_hbm, fold))
        )
    ]

    @pl.when(g == 0)
    def _():
        for copy in nozzle_args:
            copy.start()

    @pl.when(g == 1)
    def _():
        for copy in spray_args:
            copy.start()

    barrier = pltpu.get_barrier_semaphore()
    sides = [
        (s > 0, (g, s - 1, p)),
        (s < n_slab - 1, (g, s + 1, p)),
        (p > 0, (g, s, p - 1)),
        (p < n_plane - 1, (g, s, p + 1)),
    ]
    near = 0
    for there, target in sides:
        near = near + there.astype(jnp.int32)

        @pl.when(there)
        def _():
            pl.semaphore_signal(barrier, inc=1, device_id=target, device_id_type=MESH)

    @pl.when(g == 1)
    def _():
        @pl.loop(0, owners)
        def _(o):
            pl.semaphore_signal(
                barrier, inc=1, device_id=(0, o // n_plane, o % n_plane), device_id_type=MESH
            )

    load.wait()

    def lines(a, h):
        return pl.ds(a // 8 * 16 + h * 8 + a % 8, sections, stride=2 * ca)

    def gather_row(ref, a):
        return jnp.concatenate([ref[lines(a, h), :] for h in range(2)], axis=1)

    def half(ref, h):
        return ref[...].reshape(rows // 8, 2, 8, LANES)[:, h].reshape(rows, LANES)

    for a in (0, ca - 1):
        tbuf[a + 1] = gather_row(fbuf, a)

    def halo(kind, target):
        source, landing = (
            (tbuf.at[ca], tbuf.at[0]),
            (tbuf.at[1], tbuf.at[ca + 1]),
            (cols_out.at[1], cols_in.at[0]),
            (cols_out.at[0], cols_in.at[1]),
        )[kind]
        return pltpu.make_async_remote_copy(
            src_ref=source,
            dst_ref=landing,
            send_sem=halo_send.at[kind],
            recv_sem=halo_recv.at[kind],
            device_id=target,
            device_id_type=MESH,
        )

    pl.semaphore_wait(barrier, near + jnp.where(g == 0, owners, 0))

    outgoing = (sides[1], sides[0], sides[3], sides[2])
    def start_halo(kinds):
        for kind in kinds:

            @pl.when(outgoing[kind][0])
            def _():
                halo(kind, outgoing[kind][1]).start()

    start_halo((0, 1))

    lane = lax.broadcasted_iota(jnp.int32, (8, LANES), 1)
    for h, at in ((0, 0), (1, LANES - 1)):
        select = (lane == at).astype(BF16)
        cols_out[h] = dot_last(select, half(fbuf, h).astype(BF16))[0:1]

    start_halo((2, 3))

    @pl.loop(1, ca - 1)
    def _(a):
        tbuf[a + 1] = gather_row(fbuf, a)

    for kind, landing in enumerate((tbuf.at[0], tbuf.at[ca + 1], cols_in.at[0], cols_in.at[1])):

        @pl.when(jnp.logical_not(sides[kind][0]))
        def _():
            landing[...] = jnp.zeros(landing.shape, F32)

    def finish_halo():
        for kind in range(4):

            @pl.when(outgoing[kind][0])
            def _():
                halo(kind, outgoing[kind][1]).wait_send()

            @pl.when(sides[kind][0])
            def _():
                halo(kind, outgoing[kind][1]).wait_recv()

        sub = lax.broadcasted_iota(jnp.int32, (16, cb), 0)
        lanes = lax.broadcasted_iota(jnp.int32, (16, cb), 1)
        stack = jnp.concatenate([cols_in[0], cols_in[1], jnp.zeros((14, rows), F32)], axis=0)
        place = jnp.logical_or(
            jnp.logical_and(sub == 0, lanes == 0), jnp.logical_and(sub == 1, lanes == cb - 1)
        ).astype(BF16)
        placed = jnp.dot(stack.T.astype(BF16), place, preferred_element_type=F32)
        for h in range(2):
            hbuf[h] = placed[:, h * LANES : (h + 1) * LANES]

    col_lane = lax.broadcasted_iota(jnp.int32, (sections, cb), 1)
    col_row = lax.broadcasted_iota(jnp.int32, (sections, cb), 0)

    def column_halo(a):
        return jnp.concatenate(
            [hbuf[h, pl.ds(a, sections, stride=ca), :] for h in range(2)], axis=1
        )

    def neighbours(a):
        c = tbuf[a + 1]
        up = tbuf[a]
        left = jnp.where(col_lane == 0, 0.0, pltpu.roll(c, 1, 1))
        right = jnp.where(col_lane == cb - 1, 0.0, pltpu.roll(c, cb - 1, 1))
        lap = up + tbuf[a + 2] + (left + right + column_halo(a)) - 4.0 * c
        return c, up, lap

    def scatter_row(a, value):
        for h in range(2):
            obuf[lines(a, h), :] = value[:, h * LANES : (h + 1) * LANES]

    store = pltpu.make_async_copy(obuf, out_hbm, out_sem)

    @pl.when(g == 0)
    def _():
        for copy in nozzle_args:
            copy.wait()
        owner = owner_ref[...]
        slots = []
        below = lax.broadcasted_iota(jnp.int32, (256, 256), 0)
        after = lax.broadcasted_iota(jnp.int32, (256, 256), 1)
        upto = (below <= after).astype(BF16)
        names = lax.broadcasted_iota(jnp.int32, (owners, 256), 0)
        carry = jnp.zeros((owners, 1), F32)
        for j in range(exit_rows // 256):
            hit = (owner[:, j * 256 : (j + 1) * 256] == names).astype(F32)
            count = jnp.dot(hit.astype(BF16), upto, preferred_element_type=F32) + carry
            slots.append(jnp.sum(hit * (count - 1.0), axis=0, keepdims=True))
            carry = count[:, 255:256]
        slot = jnp.concatenate(slots, axis=1)
        cell = cell_ref[...]
        across = jnp.bitwise_and(cell, cb - 1)
        along = jnp.right_shift(cell, cb.bit_length() - 1)
        par[4:5] = pid_ref[...].astype(F32)
        par[5:6] = along.astype(F32)
        par[6:7] = across.astype(F32)
        par[7:8] = jnp.zeros((1, exit_rows), F32)
        places = lax.broadcasted_iota(jnp.int32, (SLOTS, exit_rows), 0).astype(F32)
        in_slot[...] = (slot == places).astype(BF16)
        group = 16
        label = jnp.right_shift(lax.broadcasted_iota(jnp.int32, (group * 8, exit_rows), 0), 3)

        @pl.loop(0, owners // group)
        def _(b):
            picks[pl.ds(pl.multiple_of(b * group * 8, group * 8), group * 8)] = (
                owner == label + b * group
            ).astype(BF16)

        halve = jnp.where(
            jnp.right_shift(lax.broadcasted_iota(jnp.int32, (cb, cb // 2), 0), 1)
            == lax.broadcasted_iota(jnp.int32, (cb, cb // 2), 1),
            0.25,
            0.0,
        ).astype(BF16)

        finish_halo()

        layers = sections // 4
        plane_row = lax.broadcasted_iota(jnp.int32, (ca, cb), 0)
        plane_lane = lax.broadcasted_iota(jnp.int32, (ca, cb), 1)

        def plane(k):
            tiles = fbuf[pl.ds(k * 2 * ca, 2 * ca), :].reshape(ca // 8, 2, 8, LANES)
            return jnp.concatenate([tiles[:, h].reshape(ca, LANES) for h in range(2)], axis=1)

        def plane_lap(c, k):
            up = jnp.where(plane_row == 0, tbuf[0, k : k + 1], pltpu.roll(c, 1, 0))
            down = jnp.where(
                plane_row == ca - 1, tbuf[ca + 1, k : k + 1], pltpu.roll(c, ca - 1, 0)
            )
            left = jnp.where(plane_lane == 0, 0.0, pltpu.roll(c, 1, 1))
            right = jnp.where(plane_lane == cb - 1, 0.0, pltpu.roll(c, cb - 1, 1))
            at = pl.ds(k * ca, ca)
            halo_col = jnp.concatenate([hbuf[h, at] for h in range(2)], axis=1)
            return up + down + (left + right + halo_col) - 4.0 * c

        last = [v * layers + layers - 1 for v in range(4)]
        d, m, q, e = (plane(k) for k in last)
        if layers > 1:
            dm, dq, de = (x - plane(k - 1) for x, k in zip((m, q, e), last[1:]))
        else:
            dm, dq, de = m, q, e
        relaxing = relax_rate / (1.0 + d * d)
        exits = [
            m - cfl_nozzle * (dm + dq) + diffusion * plane_lap(m, last[1]),
            q
            + relax_step * relaxing * (e - q)
            - cfl_nozzle * dq
            + diffusion * plane_lap(q, last[2]),
            e - cfl_nozzle * de + diffusion * plane_lap(e, last[3]),
        ]
        paired = jnp.concatenate([x + pltpu.roll(x, ca - 1, 0) for x in exits], axis=0)
        hi = paired.astype(BF16)
        rest = paired - hi.astype(F32)
        mid, low = split_hi_lo(rest)
        sums = jnp.dot(
            jnp.concatenate([hi, mid, low], axis=0), halve, preferred_element_type=F32
        )
        coarse = sums[: 3 * ca] + sums[3 * ca : 6 * ca] + sums[6 * ca :]
        flux, quality, enthalpy = (coarse[v * ca : (v + 1) * ca] for v in range(3))
        strength = jnp.sqrt(1.0 + flux * flux)
        center = (sections - 1) * jax.nn.sigmoid(enthalpy - 2.0 * quality)
        for base, value in ((0, strength), (2, center)):
            hi, low = split_hi_lo(value)
            for k, part in ((base, hi.astype(F32)), (base + 1, low.astype(F32))):
                for i in range(ca // 2):
                    par[k : k + 1, i * (cb // 2) : (i + 1) * (cb // 2)] = part[2 * i : 2 * i + 1]

        values = par[...].astype(BF16)
        tiled = jnp.concatenate([values] * group, axis=0)

        @pl.loop(0, owners // group)
        def _(b):
            picked = tiled * picks[pl.ds(pl.multiple_of(b * group * 8, group * 8), group * 8)]
            packed = dot_last(picked, in_slot[...]).reshape(group, 8, SLOTS)
            send_buf[pl.ds(b * group, group)] = jnp.concatenate(
                [packed[:, :, :LANES], packed[:, :, LANES:]], axis=1
            ).astype(BF16)

            @pl.loop(0, group)
            def _(k):
                o = b * group + k
                pltpu.make_async_remote_copy(
                    src_ref=send_buf.at[o],
                    dst_ref=recv_buf.at[me],
                    send_sem=row_send.at[o],
                    recv_sem=row_recv.at[me],
                    device_id=(1, o // n_plane, o % n_plane),
                    device_id_type=MESH,
                ).start()

        @pl.loop(0, ca // CHUNK)
        def _(step):
            for t in range(CHUNK):
                a = step * CHUNK + t
                c, _, lap = neighbours(a)
                back = jnp.where(jnp.bitwise_and(col_row, layers - 1) == 0, 0.0, pltpu.roll(c, 1, 0))
                du = c - back
                d, m, q, e = (c[v * layers : (v + 1) * layers] for v in range(4))
                dm, dq, de = (du[v * layers : (v + 1) * layers] for v in (1, 2, 3))
                relaxing = relax_rate / (1.0 + d * d)
                fresh = diffusion * lap + jnp.concatenate(
                    [
                        d - cfl_nozzle * dm,
                        m - cfl_nozzle * (dm + dq),
                        q + relax_step * relaxing * (e - q) - cfl_nozzle * dq,
                        e - cfl_nozzle * de,
                    ],
                    axis=0,
                )
                scatter_row(a, fresh)

        store.start()

        @pl.loop(0, owners)
        def _(o):
            pltpu.make_async_remote_copy(
                src_ref=send_buf.at[o],
                dst_ref=recv_buf.at[me],
                send_sem=row_send.at[o],
                recv_sem=row_recv.at[me],
                device_id=(1, o // n_plane, o % n_plane),
                device_id_type=MESH,
            ).wait_send()

    @pl.when(g == 1)
    def _():
        for copy in spray_args:
            copy.wait()
        folded = jnp.dot(coal_ref[...], fold[...], preferred_element_type=F32).astype(BF16)
        evap = jnp.zeros((sections, cb), F32)
        for k in range(sections):
            evap = jnp.where(col_row == k, evap_ref[k], evap)
        speeds = 0.2 + 0.5 * col_row.astype(F32) / (sections - 1)

        finish_halo()

        @pl.loop(0, ca // CHUNK)
        def _(step):
            parts = []
            for t in range(CHUNK):
                c, up, lap = neighbours(step * CHUNK + t)
                lost = evap * c
                gained = jnp.where(
                    col_row == sections - 1, 0.0, pltpu.roll(lost, sections - 1, 0)
                )
                parts.append(c - speeds * (c - up) + diffusion * lap - lost + gained)
            moved = jnp.concatenate(parts, axis=1)
            first = jnp.dot(folded, pair_terms(moved), preferred_element_type=F32)
            middle = moved + (0.5 * collide_step) * first
            second = jnp.dot(folded, pair_terms(middle), preferred_element_type=F32)
            mixed = moved + collide_step * second
            for t in range(CHUNK):
                scatter_row(step * CHUNK + t, mixed[:, t * cb : (t + 1) * cb])

        level = lax.broadcasted_iota(jnp.int32, (sections, SLOTS), 0).astype(F32)
        index_a = lax.broadcasted_iota(jnp.int32, (ca, SLOTS), 0).astype(F32)
        index_b = lax.broadcasted_iota(jnp.int32, (cb, SLOTS), 0).astype(F32)

        @pl.loop(0, owners // SOURCES)
        def _(step):
            lefts, rights = [], []
            for t in range(SOURCES):
                o = step * SOURCES + t
                pltpu.make_async_remote_copy(
                    src_ref=send_buf.at[o],
                    dst_ref=recv_buf.at[o],
                    send_sem=row_send.at[o],
                    recv_sem=row_recv.at[o],
                    device_id=(0, s, p),
                    device_id_type=MESH,
                ).wait_recv()
                block = recv_buf[o].astype(F32)
                got = jnp.concatenate([block[:8], block[8:]], axis=1)
                strength = got[0:1] + got[1:2]
                center = got[2:3] + got[3:4]
                spread = jnp.full((1, SLOTS), width_ref[0], F32)
                for k in range(1, plumes):
                    spread = jnp.where(got[4:5] == float(k), width_ref[k], spread)
                scaled = (level - center) / spread
                weights = 1.0 / (1.0 + scaled * scaled)
                masses = strength * weights / jnp.sum(weights, axis=0, keepdims=True)
                mask = (got[5:6] == index_a).astype(BF16)
                lefts.append(
                    jnp.concatenate(
                        [
                            jnp.broadcast_to(masses[k : k + 1], (ca, SLOTS)).astype(BF16) * mask
                            for k in range(sections)
                        ],
                        axis=0,
                    )
                )
                rights.append((got[6:7] == index_b).astype(BF16))
            left = jnp.concatenate(lefts, axis=1)
            right = jnp.concatenate(rights, axis=1)
            added = dot_last(left, right)
            tiles = jnp.stack(
                [added[:, h * LANES : (h + 1) * LANES].reshape(rows // 8, 8, LANES) for h in range(2)],
                axis=1,
            )
            obuf[...] += tiles.reshape(2 * rows, LANES)

        store.start()

    store.wait()


def settle(held_hbm, out_hbm, buf, in_sem, out_sem):
    pieces = in_sem.shape[0]
    size = buf.shape[0] // pieces
    parts = [pl.ds(k * size, size) for k in range(pieces)]
    reads = [
        pltpu.make_async_copy(held_hbm.at[at], buf.at[at], in_sem.at[k])
        for k, at in enumerate(parts)
    ]
    writes = [
        pltpu.make_async_copy(buf.at[at], out_hbm.at[at], out_sem.at[k])
        for k, at in enumerate(parts)
    ]
    for read in reads:
        read.start()
    for read, write in zip(reads, writes):
        read.wait()
        write.start()
    for write in writes:
        write.wait()


def body(n_slab, n_plane, fields, evap_rates, coal_kernel, plume_width, owner_map, deposit_cell, plume_ids):
    _, sections, ca, cb = fields.shape
    exit_rows = owner_map.shape[1]
    owners = n_slab * n_plane
    rows = sections * ca
    fold = jnp.asarray(fold_matrix(sections), BF16)
    kept = fold.shape[1]
    hbm = pl.BlockSpec(memory_space=pl.ANY)
    out = pl.pallas_call(
        functools.partial(kernel, n_slab, n_plane, sections, ca, cb, exit_rows),
        out_shape=jax.ShapeDtypeStruct((2 * rows, LANES), F32),
        in_specs=[hbm] * 8,
        out_specs=hbm,
        scratch_shapes=[
            pltpu.VMEM((2 * rows, LANES), F32),
            pltpu.VMEM((ca + 2, sections, cb), F32),
            pltpu.VMEM((2, rows, LANES), F32),
            pltpu.VMEM((2 * rows, LANES), F32),
            pltpu.VMEM((sections * sections, kept), BF16),
            pltpu.VMEM((2, 1, rows), F32),
            pltpu.VMEM((2, 1, rows), F32),
            pltpu.VMEM((8, exit_rows), F32),
            pltpu.VMEM((owners, 16, LANES), BF16),
            pltpu.VMEM((owners, 16, LANES), BF16),
            pltpu.SMEM(evap_rates.shape, F32),
            pltpu.VMEM(coal_kernel.shape, BF16),
            pltpu.SMEM(plume_width.shape, F32),
            pltpu.VMEM((1, exit_rows), jnp.int32),
            pltpu.VMEM((1, exit_rows), jnp.int32),
            pltpu.VMEM((1, exit_rows), jnp.int32),
            pltpu.VMEM((owners * 8, exit_rows), BF16),
            pltpu.VMEM((SLOTS, exit_rows), BF16),
            pltpu.SemaphoreType.DMA,
            pltpu.SemaphoreType.DMA,
            pltpu.SemaphoreType.DMA((4,)),
            pltpu.SemaphoreType.DMA((4,)),
            pltpu.SemaphoreType.DMA((4,)),
            pltpu.SemaphoreType.DMA((owners,)),
            pltpu.SemaphoreType.DMA((owners,)),
        ],
        compiler_params=pltpu.CompilerParams(
            collective_id=0, has_side_effects=True, vmem_limit_bytes=VMEM_BYTES
        ),
    )(
        fields.reshape(rows // 8, 8, 2, LANES).transpose(0, 2, 1, 3).reshape(2 * rows, LANES), evap_rates, coal_kernel, fold, plume_width,
        owner_map, deposit_cell, plume_ids,
    )
    out = pl.pallas_call(
        settle,
        out_shape=jax.ShapeDtypeStruct((2 * rows, LANES), F32),
        in_specs=[hbm],
        out_specs=hbm,
        scratch_shapes=[
            pltpu.VMEM((2 * rows, LANES), F32),
            pltpu.SemaphoreType.DMA((4,)),
            pltpu.SemaphoreType.DMA((4,)),
        ],
        compiler_params=pltpu.CompilerParams(vmem_limit_bytes=VMEM_BYTES),
    )(out)
    out = out.reshape(rows // 8, 2, 8, LANES).transpose(0, 2, 1, 3)
    return out.reshape(1, sections, ca, cb)


def solution(mesh):
    return jax.shard_map(
        functools.partial(body, mesh.shape["slab"], mesh.shape["plane"]),
        mesh=mesh,
        in_specs=(
            P("group", None, "slab", "plane"),
            P(),
            P(),
            P(),
            P(("slab", "plane"), None),
            P(("slab", "plane"), None),
            P(("slab", "plane"), None),
        ),
        out_specs=P("group", None, "slab", "plane"),
        check_vma=False,
    )
```
